256 devices in a mesh: red: 32 (over y, x, core), rep: 8 (over z).
Axes of the slice: x: 4, y: 4, z: 8, core: 2. Of those that a mesh axis runs over, the one named last changes fastest.
Arguments:
- amplitudes: bfloat16 [1024, 524288], P('red', 'rep'), may hold values from -6 to 6
- integrals: bfloat16 [524288, 2048], P(('red', 'rep')), may hold values from -0.03125 to 0.03125
- tile_perm: int32 [8, 32], P('rep'), may hold values from 0 to 31, each once within a row
- occ_index: int32 [4, 2, 16], replicated, may hold values from 0 to 124
- occ_energy: float32 [125], replicated, may hold values from -2 to -0.3
- block_sizes: int32 [8], replicated, may hold values from 64 to 832, as said below
- slab_irrep: int32 [1], replicated, may hold values from 0 to 7
- virt_energy: float32 [2048], replicated, may hold values from 0.2 to 4
Outputs:
- update: float32 [1024, 2048], P('red', 'rep')
The draws below stay inside these ranges and needn't reach their ends.
Inputs may be any that keep to these rules, and one draw needn't show every extreme that they name: `block_sizes`: each a multiple of 64, together 2048. `tile_perm`: each row is a permutation.
All inputs are finite; a program needn't handle non-finite values.
Results may differ from the reference program's by a relative error of at most 0.0003.
Values may be sent and summed in bfloat16 or wider, within the bound.
No kernel may reach another device: no remote copies, remote signals or barrier semaphores. Data moves between devices by JAX's collectives and lax.ppermute only.
A program may use at most 64 MiB of HBM per device.

```python
import math
import jax
import jax.numpy as jnp
from jax import lax

NOCC = 125
NVIRT = 2048
NIRREP = 8
SUB = 64
A_SLAB = 32
OT = 16
NPAIR = 4
TILE = 2048
IJ = 1024
AB = 2048
KPAIRS = 524288
N_RED = 32
N_REP = 8


def draw_block_sizes(key, part):
    key = jax.random.fold_in(key, 11)
    extra = NVIRT // SUB - NIRREP
    big_units = extra - extra // 2
    rest_units = extra // 2
    key_big, key_rest = jax.random.split(key)
    largest = jax.random.randint(key_big, (), 0, NIRREP)
    picks = jax.random.randint(key_rest, (max(rest_units, 1),), 0, NIRREP - 1)
    owners = (largest + 1 + picks) % NIRREP
    valid = (jnp.arange(max(rest_units, 1)) < rest_units).astype(jnp.int32)
    counts = jnp.sum((owners[:, None] == jnp.arange(NIRREP)[None, :]).astype(jnp.int32) * valid[:, None], axis=0)
    counts = counts + jnp.where(jnp.arange(NIRREP) == largest, big_units, 0)
    return ((counts + 1) * SUB).astype(jnp.int32)


def set_ends(result, stream_key, smallest, high):
    extent = result.shape
    spot = [jax.random.randint(jax.random.fold_in(stream_key, axis), (), 0, extent[axis]) for axis in range(len(extent))]
    result = result.at[tuple(spot)].set(smallest)
    longest = extent.index(max(extent))
    spot[longest] = (spot[longest] + 1) % extent[longest]
    return result.at[tuple(spot)].set(high)


def with_spikes(entries, rng, source, target, parts, factor):
    def block_of(dim):
        return (jnp.arange(entries.shape[dim]) // (entries.shape[dim] // parts)).reshape((-1,) + (1,) * (entries.ndim - 1 - dim))

    near = jax.random.permutation(rng, parts)[block_of(target)]
    far = (block_of(target) + parts // 2) % parts
    return jnp.where((block_of(source) == near) | (block_of(source) == far), factor * entries, entries)


def level_of(key, dims, pieces, least, high):
    factor_of, own = 1.0, jax.random.fold_in(key, 6)
    for position, blocks in pieces:
        draws = jnp.exp(jax.random.uniform(jax.random.fold_in(own, position), (blocks,), jnp.float32, least / len(pieces), high / len(pieces)))
        factor_of = factor_of * jnp.repeat(draws, dims[position] // blocks).reshape([-1 if axis == position else 1 for axis in range(len(dims))])
    return factor_of


def scatter_about(own_key, dims, scale, reach, pieces=(), kind=jnp.bfloat16):
    factor_of = level_of(own_key, dims, pieces, -0.22, 0.18) if pieces else 1.0
    entries = jax.random.normal(own_key, dims, jnp.float32) * scale * factor_of
    return jnp.minimum(jnp.maximum(entries, -reach), reach).astype(kind)


def bell_draw_with(rng, shape, width, most, cuts, heavy, held_as=jnp.bfloat16):
    drawn = width * jax.random.normal(rng, shape, jnp.float32)
    if cuts:
        drawn = drawn * level_of(rng, shape, cuts, -0.22, 0.18)
    return jnp.clip(with_spikes(drawn, jax.random.fold_in(rng, 3), *heavy), -most, most).astype(held_as)


def setup_inputs(seed: int = 0) -> dict:
    streams_of = jax.random.split(jax.random.key(seed), 9)
    return {
        "amplitudes": scatter_about(streams_of[0], (IJ, KPAIRS), 1.0, 6.0, ((0, 32), (1, 8))),
        "integrals": bell_draw_with(streams_of[1], (KPAIRS, AB), KPAIRS ** -0.5, 0.03125, ((0, 256),), (0, 1, 256, 6.0)),
        "tile_perm": jax.vmap(lambda own: jax.random.permutation(own, N_RED))(jax.random.split(streams_of[2], N_REP)).reshape((N_REP, N_RED)).astype(jnp.int32),
        "occ_index": set_ends(jax.random.randint(streams_of[3], (NPAIR, 2, OT), 0, NOCC), jax.random.fold_in(streams_of[3], 1), 0, NOCC - 1).astype(jnp.int32),
        "occ_energy": jnp.clip(jax.random.uniform(streams_of[4], (NOCC,), jnp.float32, -2.0, -0.3), -2.0, -0.3),
        "block_sizes": draw_block_sizes(jax.random.fold_in(streams_of[8], 71), 0),
        "slab_irrep": jax.random.randint(streams_of[6], (1,), 0, NIRREP).astype(jnp.int32),
        "virt_energy": jnp.clip(jnp.exp(jax.random.uniform(streams_of[7], (NVIRT,), jnp.float32, math.log(0.2), math.log(4.0))), 0.2, 4.0),
    }


def reference(amplitudes, integrals, tile_perm, occ_index, occ_energy, block_sizes, slab_irrep, virt_energy):
    blocks = amplitudes.reshape(IJ, N_REP, N_RED, TILE)
    column_ids = jnp.arange(N_REP, dtype=jnp.int32)[:, None]
    picked = blocks[:, column_ids, tile_perm, :]
    picked = jnp.transpose(picked, (0, 2, 1, 3)).reshape(IJ, N_RED * N_REP * TILE)
    ladder = jnp.dot(picked, integrals, preferred_element_type=jnp.float32)
    e_left = occ_energy[occ_index[:, 0, :]]
    e_right = occ_energy[occ_index[:, 1, :]]
    pair_energy = (e_left[:, :, None] + e_right[:, None, :]).reshape(IJ)
    irreps = jnp.arange(NIRREP, dtype=jnp.int32)
    start = jnp.sum(jnp.where(irreps < slab_irrep[0], block_sizes, 0)).astype(jnp.int32)
    e_a = lax.dynamic_slice(virt_energy, (start,), (A_SLAB,))
    e_b = lax.dynamic_slice(virt_energy, (start,), (SUB,))
    slab_energy = (e_a[:, None] + e_b[None, :]).reshape(AB)
    return ladder / (pair_energy[:, None] - slab_energy[None, :])
```

```python
import jax
import jax.numpy as jnp
from jax import lax
from jax.experimental import pallas as pl
from jax.experimental.pallas import tpu as pltpu
from jax.sharding import Mesh, PartitionSpec as P

SUB = 64
A_SLAB = 32
N_Y, N_X, N_CORE, N_REP = 4, 4, 2, 8
N_RED = N_Y * N_X * N_CORE
RED = ("y", "x", "core")
STEPS = (("x", 1), ("y", 1), ("x", 3), ("y", 3))
PIECES = 4


def step_bits(axis, mask):
    return mask * (N_CORE if axis == "x" else N_CORE * N_X)


def piece_steps(piece):
    return tuple(STEPS[(piece + k) % 4] for k in range(4))


def offsets(piece):
    steps = piece_steps(piece)
    out = []
    for pos in range(16):
        off = 0
        for k in range(4):
            if (pos >> (3 - k)) & 1:
                off ^= step_bits(*steps[k])
        out.append(off)
    return out


def swap(x, axis, mask, size):
    return lax.ppermute(x, axis, [(i, i ^ mask) for i in range(size)])


def pack_kernel(perm_ref, amp_ref, out_ref, sems):
    tile = out_ref.shape[2]

    def copy(r):
        cols = pl.ds(pl.multiple_of(perm_ref[0, r] * tile, tile), tile)
        return pltpu.make_async_copy(amp_ref.at[:, cols], out_ref.at[r], sems.at[r])

    for r in range(N_RED):
        copy(r).start()
    for r in range(N_RED):
        copy(r).wait()


def pack(amplitudes, tile_perm, tile):
    rows = amplitudes.shape[0]
    return pl.pallas_call(
        pack_kernel,
        out_shape=jax.ShapeDtypeStruct((N_RED, rows, tile), amplitudes.dtype),
        in_specs=[pl.BlockSpec(memory_space=pltpu.SMEM), pl.BlockSpec(memory_space=pl.ANY)],
        out_specs=pl.BlockSpec(memory_space=pl.ANY),
        scratch_shapes=[pltpu.SemaphoreType.DMA((N_RED,))],
        cost_estimate=pl.CostEstimate(
            flops=0, bytes_accessed=4 * amplitudes.size, transcendentals=0
        ),
    )(tile_perm, amplitudes)


def dot_kernel(half, where_ref, amp_ref, b_ref, out_ref, lhs, sems):
    rows = amp_ref.shape[1]
    step = pl.program_id(0)

    def copy(piece, pos):
        block = where_ref[0] ^ (offsets(piece)[pos] | half)
        return pltpu.make_async_copy(
            amp_ref.at[block],
            lhs.at[piece % 2, pl.ds(pos * rows, rows), :],
            sems.at[piece % 2, pos],
        )

    for piece in range(PIECES):

        @pl.when(step == 2 * piece)
        def _():
            if piece == 0:
                for pos in range(16):
                    copy(0, pos).start()
            if piece + 1 < PIECES:
                for pos in range(16):
                    copy(piece + 1, pos).start()
            for pos in range(16):
                copy(piece, pos).wait()

    slot = lax.rem(step // 2, 2)
    out_ref[0] = jnp.dot(lhs[slot], b_ref[...], preferred_element_type=jnp.float32)


def dot_half(half, where, amp, b):
    n_red, rows, tile = amp.shape
    width = b.shape[1] // N_REP
    m = rows * 16
    return pl.pallas_call(
        lambda *refs: dot_kernel(half, *refs),
        out_shape=jax.ShapeDtypeStruct((PIECES, m, 2 * width), jnp.float32),
        grid_spec=pltpu.PrefetchScalarGridSpec(
            num_scalar_prefetch=1,
            grid=(2 * PIECES,),
            in_specs=[
                pl.BlockSpec(memory_space=pl.ANY),
                pl.BlockSpec((tile, width), lambda s, w: (0, s ^ w[1])),
            ],
            out_specs=pl.BlockSpec((1, m, width), lambda s, w: (s // 2, 0, s % 2)),
            scratch_shapes=[
                pltpu.VMEM((2, m, tile), amp.dtype),
                pltpu.SemaphoreType.DMA((2, 16)),
            ],
        ),
        compiler_params=pltpu.CompilerParams(vmem_limit_bytes=24 * 1024 * 1024),
        cost_estimate=pl.CostEstimate(
            flops=2 * m * tile * b.shape[1],
            bytes_accessed=2 * tile * b.shape[1] + 2 * m * tile + 4 * m * b.shape[1],
            transcendentals=0,
        ),
    )(where, amp, b)


def body(
    amplitudes, integrals, tile_perm, occ_index, occ_energy, block_sizes, slab_irrep, virt_energy
):
    rows = amplitudes.shape[0]
    tile = integrals.shape[0]
    columns = integrals.shape[1] // N_REP
    red = (lax.axis_index("y") * N_X + lax.axis_index("x")) * N_CORE + lax.axis_index("core")
    rep = lax.axis_index("rep")
    where = jnp.stack([red, rep]).astype(jnp.int32)
    ordered = pack(amplitudes, tile_perm, tile)
    received = lax.all_to_all(ordered, RED, split_axis=0, concat_axis=0, tiled=True)
    away = dot_half(1, where, received, integrals)
    arrived = swap(away, "core", 1, 2)
    home = dot_half(0, where, received, integrals)

    terms = [[home[p], arrived[p]] for p in range(PIECES)]
    n = 16 * rows
    for k in range(4):
        n //= 2
        sent = [sum(t[n : 2 * n] for t in terms[p][1:]) + terms[p][0][n : 2 * n] for p in range(PIECES)]
        for p in range(PIECES):
            axis, mask = piece_steps(p)[k]
            got = swap(sent[p], axis, mask, 4)
            terms[p] = [t[:n] for t in terms[p]] + [got]
    pieces = []
    for p in range(PIECES):
        total = terms[p][-1]
        for t in terms[p][:-1]:
            total = total + t
        pieces.append(total)
    got = swap(jnp.concatenate([pieces[2], pieces[3]], axis=1), "rep", 4, N_REP)
    pieces = [pieces[0] + got[:, : 2 * columns], pieces[1] + got[:, 2 * columns :]]
    got = swap(pieces[1], "rep", 2, N_REP)
    near = pieces[0] + got
    got = swap(near[:, columns:], "rep", 1, N_REP)
    ladder = near[:, :columns] + got

    n_occ = occ_energy.shape[0]
    matches = occ_index[:, :, :, None] == jnp.arange(n_occ, dtype=jnp.int32)[None, None, None, :]
    orbital_e = jnp.sum(jnp.where(matches, occ_energy[None, None, None, :], 0.0), axis=-1)
    pair_energy = (orbital_e[:, 0, :, None] + orbital_e[:, 1, None, :]).reshape(-1)
    row_energy = lax.dynamic_slice_in_dim(pair_energy, red * rows, rows, 0)
    irreps = jnp.arange(block_sizes.shape[0], dtype=jnp.int32)
    start = jnp.sum(jnp.where(irreps < slab_irrep[0], block_sizes, 0))
    e_a = lax.dynamic_slice(virt_energy, (start,), (A_SLAB,))
    e_b = lax.dynamic_slice(virt_energy, (start,), (SUB,))
    slab_energy = (e_a[:, None] + e_b[None, :]).reshape(-1)
    col_energy = lax.dynamic_slice_in_dim(slab_energy, rep * columns, columns, 0)
    return ladder / (row_energy[:, None] - col_energy[None, :])


def solution(mesh):
    grid = Mesh(mesh.devices.reshape(N_Y, N_X, N_CORE, N_REP), RED + ("rep",))
    placed = (P(RED, "rep"), P(RED + ("rep",), None), P("rep", None), P(), P(), P(), P(), P())
    return jax.shard_map(
        body, mesh=grid, in_specs=placed, out_specs=P(RED, "rep"), check_vma=False
    )
```

```python
import jax
import jax.numpy as jnp
from jax import lax
from jax.experimental import pallas as pl
from jax.experimental.pallas import tpu as pltpu
from jax.sharding import Mesh, PartitionSpec as P

SUB = 64
A_SLAB = 32
N_Y, N_X, N_CORE, N_REP = 4, 4, 2, 8
N_RED = N_Y * N_X * N_CORE
RED = ("y", "x", "core")
STRIDE = {"x": N_CORE, "y": N_CORE * N_X}
ORDER = (("x", "y"), ("y", "x"))
MASKS = ((1, 3), (3, 1))
MIB = 1024 * 1024
AMP_SPACE = pl.ANY


def offset(core, half, pos):
    first, second = (STRIDE[axis] for axis in ORDER[core])
    off = (pos & 3) * second
    for k, mask in enumerate(MASKS[half]):
        if (pos >> (3 - k)) & 1:
            off ^= mask * first
    return off


def pairs(turn, mask):
    return [(i, i ^ (mask * STRIDE[ORDER[i % 2][turn]])) for i in range(N_RED)]


def where_am_i():
    return (lax.axis_index("y") * N_X + lax.axis_index("x")) * N_CORE + lax.axis_index("core")


def pack_kernel(perm_ref, amp_ref, out_ref, sems):
    tile = out_ref.shape[2]

    def copy(r):
        cols = pl.ds(pl.multiple_of(perm_ref[0, r] * tile, tile), tile)
        return pltpu.make_async_copy(amp_ref.at[:, cols], out_ref.at[r], sems.at[r])

    for r in range(N_RED):
        copy(r).start()
    for r in range(N_RED):
        copy(r).wait()


def pack(amplitudes, tile_perm, tile):
    rows = amplitudes.shape[0]
    return pl.pallas_call(
        pack_kernel,
        out_shape=jax.ShapeDtypeStruct((N_RED, rows, tile), amplitudes.dtype),
        in_specs=[pl.BlockSpec(memory_space=pltpu.SMEM), pl.BlockSpec(memory_space=AMP_SPACE)],
        out_specs=pl.BlockSpec(memory_space=pltpu.VMEM),
        scratch_shapes=[pltpu.SemaphoreType.DMA((N_RED,))],
        compiler_params=pltpu.CompilerParams(vmem_limit_bytes=16 * MIB),
        cost_estimate=pl.CostEstimate(
            flops=0, bytes_accessed=4 * amplitudes.size, transcendentals=0
        ),
    )(tile_perm, amplitudes)


def dot_kernel(other, amp_ref, b_ref, out_ref, lhs):
    rows = amp_ref.shape[1]
    width = b_ref.shape[1] // N_REP
    per = N_REP // 2
    core = lax.axis_index("core") ^ other
    me = where_am_i() ^ other
    rep = lax.axis_index("rep")
    for half in range(2):
        for pos in range(16):
            block = me ^ jnp.where(core == 0, offset(0, half, pos), offset(1, half, pos))
            lhs[pos * rows : (pos + 1) * rows, :] = amp_ref[block]

        def step(k, carry):
            place = half * per + k
            source = (place // 2 + (place % 2) * per) ^ rep
            b = b_ref[:, pl.ds(pl.multiple_of(source * width, width), width)]
            cols = pl.ds(pl.multiple_of(k * width, width), width)
            out_ref[half, :, cols] = jnp.dot(lhs[...], b, preferred_element_type=jnp.float32)
            return carry

        lax.fori_loop(0, per, step, 0)


def dot_rows(other, amp, b):
    n_red, rows, tile = amp.shape
    m, half = rows * 16, b.shape[1] // 2
    vmem = pl.BlockSpec(memory_space=pltpu.VMEM)
    return pl.pallas_call(
        lambda *refs: dot_kernel(other, *refs),
        out_shape=jax.ShapeDtypeStruct((2, m, half), jnp.float32),
        in_specs=[vmem, vmem],
        out_specs=vmem,
        scratch_shapes=[pltpu.VMEM((m, tile), amp.dtype)],
        compiler_params=pltpu.CompilerParams(vmem_limit_bytes=24 * MIB),
        cost_estimate=pl.CostEstimate(
            flops=4 * m * tile * half,
            bytes_accessed=2 * b.size + 2 * m * tile + 8 * m * half,
            transcendentals=0,
        ),
    )(amp, b)


def total(terms):
    out = terms[0]
    for t in terms[1:]:
        out = out + t
    return out


def energy_gap(
    occ_index, occ_energy, block_sizes, slab_irrep, virt_energy, red, rep, rows, columns
):
    n_occ = occ_energy.shape[0]
    matches = occ_index[:, :, :, None] == jnp.arange(n_occ, dtype=jnp.int32)[None, None, None, :]
    orbital_e = jnp.sum(jnp.where(matches, occ_energy[None, None, None, :], 0.0), axis=-1)
    pair_energy = (orbital_e[:, 0, :, None] + orbital_e[:, 1, None, :]).reshape(-1)
    row_energy = lax.dynamic_slice_in_dim(pair_energy, red * rows, rows, 0)
    irreps = jnp.arange(block_sizes.shape[0], dtype=jnp.int32)
    start = jnp.sum(jnp.where(irreps < slab_irrep[0], block_sizes, 0))
    e_a = lax.dynamic_slice(virt_energy, (start,), (A_SLAB,))
    e_b = lax.dynamic_slice(virt_energy, (start,), (SUB,))
    slab_energy = (e_a[:, None] + e_b[None, :]).reshape(-1)
    col_energy = lax.dynamic_slice_in_dim(slab_energy, rep * columns, columns, 0)
    return row_energy[:, None] - col_energy[None, :]


def body(
    amplitudes, integrals, tile_perm, occ_index, occ_energy, block_sizes, slab_irrep, virt_energy
):
    rows = amplitudes.shape[0]
    tile = integrals.shape[0]
    columns = integrals.shape[1] // N_REP
    red, rep = where_am_i(), lax.axis_index("rep")
    ordered = pack(amplitudes, tile_perm, tile)
    received = lax.all_to_all(ordered, RED, split_axis=0, concat_axis=0, tiled=True)
    away = dot_rows(1, received, integrals)
    arrived = lax.ppermute(away, "core", [(0, 1), (1, 0)])
    home = dot_rows(0, received, integrals)
    n = 8 * rows
    sends = lax.optimization_barrier([home[half, n:] + arrived[half, n:] for half in range(2)])
    gots = [lax.ppermute(sends[half], RED, pairs(0, MASKS[half][0])) for half in range(2)]
    keeps = [home[half, :n] + arrived[half, :n] for half in range(2)]
    denominator = energy_gap(
        occ_index, occ_energy, block_sizes, slab_irrep, virt_energy, red, rep, rows, columns
    )
    gots, keeps, denominator = lax.optimization_barrier((gots, keeps, denominator))
    n = 4 * rows
    sends = lax.optimization_barrier([keeps[half][n:] + gots[half][n:] for half in range(2)])
    keeps = [keeps[half][:n] + gots[half][:n] for half in range(2)]
    gots = [lax.ppermute(sends[half], RED, pairs(0, MASKS[half][1])) for half in range(2)]
    gots, keeps = lax.optimization_barrier((gots, keeps))
    mine = jnp.concatenate([keeps[half] + gots[half] for half in range(2)], axis=1)
    mine = total(
        [mine[:rows]]
        + [
            lax.ppermute(mine[k * rows : (k + 1) * rows], RED, pairs(1, k))
            for k in range(1, 4)
        ]
    )
    width = 2 * columns
    mine = total(
        [mine[:, :width]]
        + [
            lax.ppermute(mine[:, k * width : (k + 1) * width], "rep", [(i, i ^ k) for i in range(N_REP)])
            for k in range(1, 4)
        ]
    )
    got = lax.ppermute(mine[:, columns:], "rep", [(i, i ^ 4) for i in range(N_REP)])
    return (mine[:, :columns] + got) / denominator


def solution(mesh):
    grid = Mesh(mesh.devices.reshape(N_Y, N_X, N_CORE, N_REP), RED + ("rep",))
    placed = (P(RED, "rep"), P(RED + ("rep",), None), P("rep", None), P(), P(), P(), P(), P())
    return jax.shard_map(
        body, mesh=grid, in_specs=placed, out_specs=P(RED, "rep"), check_vma=False
    )
```

```python
import functools

import jax
import jax.numpy as jnp
from jax import lax
from jax.experimental import pallas as pl
from jax.experimental.pallas import tpu as pltpu
from jax.sharding import Mesh, PartitionSpec as P

SUB = 64
A_SLAB = 32
N_Y, N_X, N_CORE, N_REP = 4, 4, 2, 8
N_RED = N_Y * N_X * N_CORE
RED = ("y", "x", "core")
STRIDE = {"x": N_CORE, "y": N_CORE * N_X}
ORDER = (("x", "y"), ("y", "x"))
MASKS = ((1, 3), (3, 1))
MIB = 1024 * 1024


def offset(core, half, pos):
    first, second = (STRIDE[axis] for axis in ORDER[core])
    off = (pos & 3) * second
    for k, mask in enumerate(MASKS[half]):
        if (pos >> (3 - k)) & 1:
            off ^= mask * first
    return off


def pairs(turn, mask):
    return [(i, i ^ (mask * STRIDE[ORDER[i % 2][turn]])) for i in range(N_RED)]


def where_am_i():
    return (lax.axis_index("y") * N_X + lax.axis_index("x")) * N_CORE + lax.axis_index("core")


def pack_kernel(perm_ref, amp_ref, out_ref):
    tile = out_ref.shape[2]
    for r in range(N_RED):
        cols = pl.ds(pl.multiple_of(perm_ref[0, r] * tile, tile), tile)
        out_ref[r] = amp_ref[:, cols]


def pack(amplitudes, tile_perm, tile):
    rows = amplitudes.shape[0]
    vmem = pl.BlockSpec(memory_space=pltpu.VMEM)
    return pl.pallas_call(
        pack_kernel,
        out_shape=jax.ShapeDtypeStruct((N_RED, rows, tile), amplitudes.dtype),
        in_specs=[pl.BlockSpec(memory_space=pltpu.SMEM), vmem],
        out_specs=vmem,
        compiler_params=pltpu.CompilerParams(vmem_limit_bytes=16 * MIB),
        cost_estimate=pl.CostEstimate(
            flops=0, bytes_accessed=4 * amplitudes.size, transcendentals=0
        ),
    )(tile_perm, amplitudes)


def dot_tiles(other, group, amp_ref, b_ref, lhs):
    rows = amp_ref.shape[1]
    width = b_ref.shape[1] // N_REP
    core = lax.axis_index("core") ^ other
    me = where_am_i() ^ other
    rep = lax.axis_index("rep")
    for half in range(2):
        for pos in range(16):
            block = me ^ jnp.where(core == 0, offset(0, half, pos), offset(1, half, pos))
            lhs[pos * rows : (pos + 1) * rows, :] = amp_ref[block]
        for k in range(2):
            source = (2 * group + half + 4 * k) ^ rep
            b = b_ref[:, pl.ds(pl.multiple_of(source * width, width), width)]
            cols = slice(k * width, (k + 1) * width)
            yield half, cols, jnp.dot(lhs[...], b, preferred_element_type=jnp.float32)


def away_kernel(group, amp_ref, b_ref, out_ref, lhs):
    for half, cols, out in dot_tiles(1, group, amp_ref, b_ref, lhs):
        out_ref[half, :, cols] = out


def home_kernel(group, amp_ref, b_ref, arrived_ref, far0, far1, near0, near1, lhs):
    n = far0.shape[0]
    for half, cols, out in dot_tiles(0, group, amp_ref, b_ref, lhs):
        out += arrived_ref[half, :, cols]
        (near0, near1)[half][:, cols] = out[:n]
        (far0, far1)[half][:, cols] = out[n:]


def in_vmem(kernel, shapes, *args, scratch=(), limit=24):
    vmem = pl.BlockSpec(memory_space=pltpu.VMEM)
    return pl.pallas_call(
        kernel,
        out_shape=[jax.ShapeDtypeStruct(shape, jnp.float32) for shape in shapes],
        in_specs=[vmem] * len(args),
        out_specs=[vmem] * len(shapes),
        scratch_shapes=scratch,
        compiler_params=pltpu.CompilerParams(vmem_limit_bytes=limit * MIB),
        cost_estimate=pl.CostEstimate(flops=0, bytes_accessed=0, transcendentals=0),
    )(*args)


def step_kernel(keep0, keep1, got0, got1, far0, far1, near0, near1):
    n = far0.shape[0]
    for keep, got, far, near in ((keep0, got0, far0, near0), (keep1, got1, far1, near1)):
        near[...] = keep[:n] + got[:n]
        far[...] = keep[n:] + got[n:]


def join_kernel(*refs):
    rows = refs[8].shape[0]
    quarter = refs[0].shape[1]
    for i in range(4):
        for k in range(4):
            part = slice(k * rows, (k + 1) * rows)
            refs[8 + k][:, i * quarter : (i + 1) * quarter] = refs[i][part] + refs[4 + i][part]


def spread_kernel(a, b, c, d, *outs):
    quarter = outs[0].shape[1]
    for k, out in enumerate(outs):
        cols = slice(k * quarter, (k + 1) * quarter)
        out[...] = (a[:, cols] + b[:, cols]) + (c[:, cols] + d[:, cols])


def energy_gap(
    occ_index, occ_energy, block_sizes, slab_irrep, virt_energy, red, rep, rows, columns
):
    n_occ = occ_energy.shape[0]
    matches = occ_index[:, :, :, None] == jnp.arange(n_occ, dtype=jnp.int32)[None, None, None, :]
    orbital_e = jnp.sum(jnp.where(matches, occ_energy[None, None, None, :], 0.0), axis=-1)
    pair_energy = (orbital_e[:, 0, :, None] + orbital_e[:, 1, None, :]).reshape(-1)
    row_energy = lax.dynamic_slice_in_dim(pair_energy, red * rows, rows, 0)
    irreps = jnp.arange(block_sizes.shape[0], dtype=jnp.int32)
    start = jnp.sum(jnp.where(irreps < slab_irrep[0], block_sizes, 0))
    e_a = lax.dynamic_slice(virt_energy, (start,), (A_SLAB,))
    e_b = lax.dynamic_slice(virt_energy, (start,), (SUB,))
    slab_energy = (e_a[:, None] + e_b[None, :]).reshape(-1)
    col_energy = lax.dynamic_slice_in_dim(slab_energy, rep * columns, columns, 0)
    return row_energy[:, None] - col_energy[None, :]


def body(
    amplitudes, integrals, tile_perm, occ_index, occ_energy, block_sizes, slab_irrep, virt_energy
):
    rows = amplitudes.shape[0]
    tile = integrals.shape[0]
    columns = integrals.shape[1] // N_REP
    red, rep = where_am_i(), lax.axis_index("rep")
    ordered = pack(amplitudes, tile_perm, tile)
    received = lax.all_to_all(ordered, RED, split_axis=0, concat_axis=0, tiled=True)
    m, quarter = 16 * rows, 2 * columns
    lhs = [pltpu.VMEM((m, tile), amplitudes.dtype)]
    arrived = []
    for group in range(2):
        (away,) = in_vmem(
            functools.partial(away_kernel, group),
            [(2, m, quarter)],
            received,
            integrals,
            scratch=lhs,
        )
        arrived.append(lax.ppermute(away, "core", [(0, 1), (1, 0)]))
    keeps, gots = [], []
    for group in range(2):
        far0, far1, *near = in_vmem(
            functools.partial(home_kernel, group),
            [(m // 2, quarter)] * 4,
            received,
            integrals,
            arrived[group],
            scratch=lhs,
        )
        keeps.append(near)
        gots.append([lax.ppermute(far, RED, pairs(0, MASKS[h][0])) for h, far in enumerate((far0, far1))])
    last, more = [], []
    for group in range(2):
        far0, far1, *near = in_vmem(step_kernel, [(m // 4, quarter)] * 4, *keeps[group], *gots[group])
        last += near
        more += [lax.ppermute(far, RED, pairs(0, MASKS[h][1])) for h, far in enumerate((far0, far1))]
    mine, *sends = in_vmem(join_kernel, [(rows, 4 * quarter)] * 4, *last, *more)
    gots = [lax.ppermute(send, RED, pairs(1, k + 1)) for k, send in enumerate(sends)]
    sends, occ_energy, virt_energy = lax.optimization_barrier((sends, occ_energy, virt_energy))
    denominator = energy_gap(
        occ_index, occ_energy, block_sizes, slab_irrep, virt_energy, red, rep, rows, columns
    )
    gots, denominator = lax.optimization_barrier((gots, denominator))
    mine, *sends = in_vmem(spread_kernel, [(rows, quarter)] * 4, mine, *gots)
    gots = [
        lax.ppermute(send, "rep", [(i, i ^ (k + 1)) for i in range(N_REP)])
        for k, send in enumerate(sends)
    ]
    mine = (mine + gots[0]) + (gots[1] + gots[2])
    got = lax.ppermute(mine[:, columns:], "rep", [(i, i ^ 4) for i in range(N_REP)])
    return (mine[:, :columns] + got) / denominator


def solution(mesh):
    grid = Mesh(mesh.devices.reshape(N_Y, N_X, N_CORE, N_REP), RED + ("rep",))
    placed = (P(RED, "rep"), P(RED + ("rep",), None), P("rep", None), P(), P(), P(), P(), P())
    return jax.shard_map(
        body, mesh=grid, in_specs=placed, out_specs=P(RED, "rep"), check_vma=False
    )
```

```python
import functools

import jax
import jax.numpy as jnp
from jax import lax
from jax.experimental import pallas as pl
from jax.experimental.pallas import tpu as pltpu
from jax.sharding import Mesh, PartitionSpec as P

SUB = 64
N_Y, N_X, N_CORE, N_REP = 4, 4, 2, 8
N_RED = N_Y * N_X * N_CORE
RED = ("y", "x", "core")
STRIDE = {"x": N_CORE, "y": N_CORE * N_X}
ORDER = (("x", "y"), ("y", "x"))
MASKS = ((1, 3), (3, 1))
MIB = 1024 * 1024


def offset(core, half, pos):
    first, second = (STRIDE[axis] for axis in ORDER[core])
    off = (pos & 3) * second
    for k, mask in enumerate(MASKS[half]):
        if (pos >> (3 - k)) & 1:
            off ^= mask * first
    return off


def pairs(turn, mask):
    return [(i, i ^ (mask * STRIDE[ORDER[i % 2][turn]])) for i in range(N_RED)]


def where_am_i():
    return (lax.axis_index("y") * N_X + lax.axis_index("x")) * N_CORE + lax.axis_index("core")


def pack_kernel(first_ref, amp_ref, out_ref):
    tile = out_ref.shape[2]
    for r in range(N_RED):
        cols = pl.ds(pl.multiple_of(first_ref[0, r], tile), tile)
        out_ref[r] = amp_ref[:, cols]


def pack(amplitudes, tile_perm, tile):
    rows = amplitudes.shape[0]
    vmem = pl.BlockSpec(memory_space=pltpu.VMEM)
    return pl.pallas_call(
        pack_kernel,
        out_shape=jax.ShapeDtypeStruct((N_RED, rows, tile), amplitudes.dtype),
        in_specs=[pl.BlockSpec(memory_space=pltpu.SMEM), vmem],
        out_specs=vmem,
        compiler_params=pltpu.CompilerParams(vmem_limit_bytes=16 * MIB),
        cost_estimate=pl.CostEstimate(
            flops=0, bytes_accessed=4 * amplitudes.size, transcendentals=0
        ),
    )(tile_perm * tile, amplitudes)


def dot_tiles(other, group, amp_ref, b_ref, lhs):
    rows = amp_ref.shape[1]
    width = b_ref.shape[1] // N_REP
    core = lax.axis_index("core") ^ other
    me = where_am_i() ^ other
    rep = lax.axis_index("rep")
    for half in range(2):
        for pos in range(16):
            block = me ^ jnp.where(core == 0, offset(0, half, pos), offset(1, half, pos))
            lhs[pos * rows : (pos + 1) * rows, :] = amp_ref[block]
        for k in range(2):
            source = (2 * group + half + 4 * k) ^ rep
            b = b_ref[:, pl.ds(pl.multiple_of(source * width, width), width)]
            cols = slice(k * width, (k + 1) * width)
            yield half, cols, jnp.dot(lhs[...], b, preferred_element_type=jnp.float32)


def away_kernel(group, amp_ref, b_ref, out_ref, lhs):
    for half, cols, out in dot_tiles(1, group, amp_ref, b_ref, lhs):
        out_ref[half, :, cols] = out


def home_kernel(group, amp_ref, b_ref, arrived_ref, far0, far1, near0, near1, lhs):
    n = far0.shape[0]
    for half, cols, out in dot_tiles(0, group, amp_ref, b_ref, lhs):
        out += arrived_ref[half, :, cols]
        (near0, near1)[half][:, cols] = out[:n]
        (far0, far1)[half][:, cols] = out[n:]


def in_vmem(kernel, shapes, *args, scratch=(), limit=24):
    vmem = pl.BlockSpec(memory_space=pltpu.VMEM)
    return pl.pallas_call(
        kernel,
        out_shape=[jax.ShapeDtypeStruct(shape, jnp.float32) for shape in shapes],
        in_specs=[vmem] * len(args),
        out_specs=[vmem] * len(shapes),
        scratch_shapes=scratch,
        compiler_params=pltpu.CompilerParams(vmem_limit_bytes=limit * MIB),
        cost_estimate=pl.CostEstimate(flops=0, bytes_accessed=0, transcendentals=0),
    )(*args)


def step_kernel(keep0, keep1, got0, got1, far0, far1, near0, near1):
    n = far0.shape[0]
    for keep, got, far, near in ((keep0, got0, far0, near0), (keep1, got1, far1, near1)):
        near[...] = keep[:n] + got[:n]
        far[...] = keep[n:] + got[n:]


def join_kernel(keep0, keep1, got0, got1, *outs):
    rows = outs[0].shape[0]
    quarter = keep0.shape[1]
    for k, out in enumerate(outs):
        part = slice(k * rows, (k + 1) * rows)
        out[:, :quarter] = keep0[part] + got0[part]
        out[:, quarter:] = keep1[part] + got1[part]


def sum_kernel(a, b, c, d, left, right):
    n = left.shape[1]
    left[...] = (a[:, :n] + b[:, :n]) + (c[:, :n] + d[:, :n])
    right[...] = (a[:, n:] + b[:, n:]) + (c[:, n:] + d[:, n:])


def energy_kernel(occ_index, occ_energy, block_sizes, slab_irrep, virt_energy, out_ref):
    rows, columns = out_ref.shape
    tile = occ_index.shape[2]
    red, rep = where_am_i(), lax.axis_index("rep")
    row = lax.broadcasted_iota(jnp.int32, (rows, columns), 0)
    column = lax.broadcasted_iota(jnp.int32, (1, columns), 1)
    pair, first = red * rows // (tile * tile), red * rows % (tile * tile) // tile
    left = jnp.zeros((rows, columns), jnp.float32)
    for i in range(rows // tile):
        left = jnp.where(row // tile == i, occ_energy[occ_index[pair, 0, first + i]], left)
    right = jnp.zeros((rows, columns), jnp.float32)
    for j in range(tile):
        right = jnp.where(row % tile == j, occ_energy[occ_index[pair, 1, j]], right)
    start = 0
    for h in range(block_sizes.shape[0]):
        start += jnp.where(h < slab_irrep[0], block_sizes[h], 0)
    e_a = jnp.zeros((1, columns), jnp.float32)
    for a in range(columns // SUB):
        e_a = jnp.where(column // SUB == a, virt_energy[start + rep * (columns // SUB) + a], e_a)
    e_b = jnp.zeros((1, columns), jnp.float32)
    for b in range(SUB):
        e_b = jnp.where(column % SUB == b, virt_energy[start + b], e_b)
    out_ref[...] = (left + right) - (e_a + e_b)


def energy_gap(rows, columns, *args):
    return pl.pallas_call(
        energy_kernel,
        out_shape=jax.ShapeDtypeStruct((rows, columns), jnp.float32),
        in_specs=[pl.BlockSpec(memory_space=pltpu.SMEM)] * len(args),
        out_specs=pl.BlockSpec(memory_space=pltpu.VMEM),
    )(*args)


def body(
    amplitudes, integrals, tile_perm, occ_index, occ_energy, block_sizes, slab_irrep, virt_energy
):
    rows = amplitudes.shape[0]
    tile = integrals.shape[0]
    columns = integrals.shape[1] // N_REP
    ordered = pack(amplitudes, tile_perm, tile)
    received = lax.all_to_all(ordered, RED, split_axis=0, concat_axis=0, tiled=True)
    m, quarter = 16 * rows, 2 * columns
    lhs = [pltpu.VMEM((m, tile), amplitudes.dtype)]
    arrived = []
    for group in range(2):
        (away,) = in_vmem(
            functools.partial(away_kernel, group),
            [(2, m, quarter)],
            received,
            integrals,
            scratch=lhs,
        )
        arrived.append(lax.ppermute(away, "core", [(0, 1), (1, 0)]))
    keeps, gots = [], []
    for group in range(2):
        far0, far1, *near = in_vmem(
            functools.partial(home_kernel, group),
            [(m // 2, quarter)] * 4,
            received,
            integrals,
            arrived[group],
            scratch=lhs,
        )
        keeps.append(near)
        gots.append([lax.ppermute(far, RED, pairs(0, MASKS[h][0])) for h, far in enumerate((far0, far1))])
    last, more = [], []
    for group in range(2):
        far0, far1, *near = in_vmem(step_kernel, [(m // 4, quarter)] * 4, *keeps[group], *gots[group])
        last.append(near)
        more.append([lax.ppermute(far, RED, pairs(0, MASKS[h][1])) for h, far in enumerate((far0, far1))])
    blocks = []
    for group in range(2):
        mine, *sends = in_vmem(join_kernel, [(rows, 2 * quarter)] * 4, *last[group], *more[group])
        gots = [lax.ppermute(send, RED, pairs(1, k + 1)) for k, send in enumerate(sends)]
        blocks += in_vmem(sum_kernel, [(rows, quarter)] * 2, mine, *gots)
    gots = [
        lax.ppermute(blocks[k], "rep", [(i, i ^ k) for i in range(N_REP)]) for k in range(1, 4)
    ]
    mine, send = in_vmem(sum_kernel, [(rows, columns)] * 2, blocks[0], *gots)
    send, occ_energy = lax.optimization_barrier((send, occ_energy))
    got = lax.ppermute(send, "rep", [(i, i ^ 4) for i in range(N_REP)])
    gap = energy_gap(
        rows, columns, occ_index, occ_energy, block_sizes, slab_irrep, virt_energy
    )
    got, gap = lax.optimization_barrier((got, gap))
    return (mine + got) / gap


def solution(mesh):
    grid = Mesh(mesh.devices.reshape(N_Y, N_X, N_CORE, N_REP), RED + ("rep",))
    placed = (P(RED, "rep"), P(RED + ("rep",), None), P("rep", None), P(), P(), P(), P(), P())
    return jax.shard_map(
        body, mesh=grid, in_specs=placed, out_specs=P(RED, "rep"), check_vma=False
    )
```

```python
import functools

import jax
import jax.numpy as jnp
from jax import lax
from jax.experimental import pallas as pl
from jax.experimental.pallas import tpu as pltpu
from jax.sharding import Mesh, PartitionSpec as P

SUB = 64
N_Y, N_X, N_CORE, N_REP = 4, 4, 2, 8
N_RED = N_Y * N_X * N_CORE
RED = ("y", "x", "core")
STRIDE = {"x": N_CORE, "y": N_CORE * N_X}
ORDER = (("x", "y"), ("y", "x"))
MASKS = ((1, 3), (3, 1))
MIB = 1024 * 1024


def offset(core, half, pos):
    first, second = (STRIDE[axis] for axis in ORDER[core])
    off = (pos & 3) * second
    for k, mask in enumerate(MASKS[half]):
        if (pos >> (3 - k)) & 1:
            off ^= mask * first
    return off


def pairs(turn, mask):
    return [(i, i ^ (mask * STRIDE[ORDER[i % 2][turn]])) for i in range(N_RED)]


def where_am_i():
    return (lax.axis_index("y") * N_X + lax.axis_index("x")) * N_CORE + lax.axis_index("core")


def pack_kernel(first_ref, amp_ref, out_ref):
    tile = out_ref.shape[2]
    for r in range(N_RED):
        cols = pl.ds(pl.multiple_of(first_ref[0, r], tile), tile)
        out_ref[r] = amp_ref[:, cols]


def pack(amplitudes, tile_perm, tile):
    rows = amplitudes.shape[0]
    vmem = pl.BlockSpec(memory_space=pltpu.VMEM)
    return pl.pallas_call(
        pack_kernel,
        out_shape=jax.ShapeDtypeStruct((N_RED, rows, tile), amplitudes.dtype),
        in_specs=[pl.BlockSpec(memory_space=pltpu.SMEM), vmem],
        out_specs=vmem,
        compiler_params=pltpu.CompilerParams(vmem_limit_bytes=16 * MIB),
        cost_estimate=pl.CostEstimate(
            flops=0, bytes_accessed=4 * amplitudes.size, transcendentals=0
        ),
    )(tile_perm * tile, amplitudes)


def dot_tiles(other, group, amp_ref, b_ref, lhs):
    rows = amp_ref.shape[1]
    width = b_ref.shape[1] // N_REP
    core = lax.axis_index("core") ^ other
    me = where_am_i() ^ other
    rep = lax.axis_index("rep")
    for half in range(2):
        for pos in range(16):
            block = me ^ jnp.where(core == 0, offset(0, half, pos), offset(1, half, pos))
            lhs[pos * rows : (pos + 1) * rows, :] = amp_ref[block]
        for k in range(2):
            source = (2 * group + half + 4 * k) ^ rep
            b = b_ref[:, pl.ds(pl.multiple_of(source * width, width), width)]
            cols = slice(k * width, (k + 1) * width)
            yield half, cols, jnp.dot(lhs[...], b, preferred_element_type=jnp.float32)


def away_kernel(group, amp_ref, b_ref, out_ref, lhs):
    for half, cols, out in dot_tiles(1, group, amp_ref, b_ref, lhs):
        out_ref[half, :, cols] = out


def encode(x, out_ref, cols):
    n = x.shape[0]
    parts = [x[i : i + 16] for i in range(0, n, 16)]
    peak = jnp.abs(parts[0])
    for part in parts[1:]:
        peak = jnp.maximum(peak, jnp.abs(part))
    exponent = jnp.floor(jnp.log2(jnp.maximum(peak, 1e-30))) + 1.0
    scale = jnp.exp2(15.0 - exponent)
    for i, part in enumerate(parts):
        code = jnp.clip(jnp.round(part * scale), -32767.0, 32767.0)
        out_ref[16 * i : 16 * (i + 1), cols] = code.astype(jnp.int32).astype(jnp.int16)
    out_ref[n : n + 16, cols] = exponent.astype(jnp.int32).astype(jnp.int16)


def decode(ref, first, rows):
    n = ref.shape[0] - 16
    exponent = ref[n : n + 16].astype(jnp.int32).astype(jnp.float32)
    scale = jnp.exp2(exponent - 15.0)
    parts = [
        ref[i : i + 16].astype(jnp.int32).astype(jnp.float32) * scale
        for i in range(first, first + rows, 16)
    ]
    return jnp.concatenate(parts, axis=0)


def home_kernel(group, amp_ref, b_ref, arrived_ref, far0, far1, near0, near1, lhs):
    n = near0.shape[0]
    for half, cols, out in dot_tiles(0, group, amp_ref, b_ref, lhs):
        out += arrived_ref[half, :, cols]
        (near0, near1)[half][:, cols] = out[:n]
        encode(out[n:], (far0, far1)[half], cols)


def in_vmem(kernel, shapes, *args, scratch=(), limit=24):
    vmem = pl.BlockSpec(memory_space=pltpu.VMEM)
    return pl.pallas_call(
        kernel,
        out_shape=[jax.ShapeDtypeStruct(*shape) for shape in shapes],
        in_specs=[vmem] * len(args),
        out_specs=[vmem] * len(shapes),
        scratch_shapes=scratch,
        compiler_params=pltpu.CompilerParams(vmem_limit_bytes=limit * MIB),
        cost_estimate=pl.CostEstimate(flops=0, bytes_accessed=0, transcendentals=0),
    )(*args)


def step_kernel(keep0, keep1, got0, got1, far0, far1, near0, near1):
    n = near0.shape[0]
    for keep, got, far, near in ((keep0, got0, far0, near0), (keep1, got1, far1, near1)):
        near[...] = keep[:n] + decode(got, 0, n)
        encode(keep[n:] + decode(got, n, n), far, slice(None))


def join_kernel(keep0, keep1, got0, got1, *outs):
    rows = outs[0].shape[0]
    quarter = keep0.shape[1]
    for k, out in enumerate(outs):
        part = slice(k * rows, (k + 1) * rows)
        out[:, :quarter] = keep0[part] + decode(got0, k * rows, rows)
        out[:, quarter:] = keep1[part] + decode(got1, k * rows, rows)


def sum_kernel(a, b, c, d, left, right):
    n = left.shape[1]
    left[...] = (a[:, :n] + b[:, :n]) + (c[:, :n] + d[:, :n])
    right[...] = (a[:, n:] + b[:, n:]) + (c[:, n:] + d[:, n:])


def energy_kernel(occ_index, occ_energy, block_sizes, slab_irrep, virt_energy, out_ref):
    rows, columns = out_ref.shape
    tile = occ_index.shape[2]
    red, rep = where_am_i(), lax.axis_index("rep")
    row = lax.broadcasted_iota(jnp.int32, (rows, columns), 0)
    column = lax.broadcasted_iota(jnp.int32, (1, columns), 1)
    pair, first = red * rows // (tile * tile), red * rows % (tile * tile) // tile
    left = jnp.zeros((rows, columns), jnp.float32)
    for i in range(rows // tile):
        left = jnp.where(row // tile == i, occ_energy[occ_index[pair, 0, first + i]], left)
    right = jnp.zeros((rows, columns), jnp.float32)
    for j in range(tile):
        right = jnp.where(row % tile == j, occ_energy[occ_index[pair, 1, j]], right)
    start = 0
    for h in range(block_sizes.shape[0]):
        start += jnp.where(h < slab_irrep[0], block_sizes[h], 0)
    e_a = jnp.zeros((1, columns), jnp.float32)
    for a in range(columns // SUB):
        e_a = jnp.where(column // SUB == a, virt_energy[start + rep * (columns // SUB) + a], e_a)
    e_b = jnp.zeros((1, columns), jnp.float32)
    for b in range(SUB):
        e_b = jnp.where(column % SUB == b, virt_energy[start + b], e_b)
    out_ref[...] = (left + right) - (e_a + e_b)


def energy_gap(rows, columns, *args):
    return pl.pallas_call(
        energy_kernel,
        out_shape=jax.ShapeDtypeStruct((rows, columns), jnp.float32),
        in_specs=[pl.BlockSpec(memory_space=pltpu.SMEM)] * len(args),
        out_specs=pl.BlockSpec(memory_space=pltpu.VMEM),
        cost_estimate=pl.CostEstimate(flops=0, bytes_accessed=0, transcendentals=0),
    )(*args)


def body(
    amplitudes, integrals, tile_perm, occ_index, occ_energy, block_sizes, slab_irrep, virt_energy
):
    rows = amplitudes.shape[0]
    tile = integrals.shape[0]
    columns = integrals.shape[1] // N_REP
    ordered = pack(amplitudes, tile_perm, tile)
    received = lax.all_to_all(ordered, RED, split_axis=0, concat_axis=0, tiled=True)
    m, quarter = 16 * rows, 2 * columns

    def stage(n):
        return [((n + 16, quarter), jnp.int16)] * 2 + [((n, quarter), jnp.float32)] * 2

    lhs = [pltpu.VMEM((m, tile), amplitudes.dtype)]
    arrived = []
    for group in range(2):
        (away,) = in_vmem(
            functools.partial(away_kernel, group),
            [((2, m, quarter), jnp.float32)],
            received,
            integrals,
            scratch=lhs,
        )
        arrived.append(lax.ppermute(away, "core", [(0, 1), (1, 0)]))
    keeps, gots = [], []
    for group in range(2):
        far0, far1, *near = in_vmem(
            functools.partial(home_kernel, group),
            stage(m // 2),
            received,
            integrals,
            arrived[group],
            scratch=lhs,
        )
        keeps.append(near)
        gots.append([lax.ppermute(far, RED, pairs(0, MASKS[h][0])) for h, far in enumerate((far0, far1))])
    keeps[1], occ_energy = lax.optimization_barrier((keeps[1], occ_energy))
    gap = energy_gap(
        rows, columns, occ_index, occ_energy, block_sizes, slab_irrep, virt_energy
    )
    gots[0], gap = lax.optimization_barrier((gots[0], gap))
    last, more = [], []
    for group in range(2):
        far0, far1, *near = in_vmem(step_kernel, stage(m // 4), *keeps[group], *gots[group])
        last.append(near)
        more.append([lax.ppermute(far, RED, pairs(0, MASKS[h][1])) for h, far in enumerate((far0, far1))])
    blocks = []
    for group in range(2):
        mine, *sends = in_vmem(join_kernel, [((rows, 2 * quarter), jnp.float32)] * 4, *last[group], *more[group])
        gots = [lax.ppermute(send, RED, pairs(1, k + 1)) for k, send in enumerate(sends)]
        blocks += in_vmem(sum_kernel, [((rows, quarter), jnp.float32)] * 2, mine, *gots)
    gots = [
        lax.ppermute(blocks[k], "rep", [(i, i ^ k) for i in range(N_REP)]) for k in range(1, 4)
    ]
    mine, send = in_vmem(sum_kernel, [((rows, columns), jnp.float32)] * 2, blocks[0], *gots)
    got = lax.ppermute(send, "rep", [(i, i ^ 4) for i in range(N_REP)])
    return (mine + got) / gap


def solution(mesh):
    grid = Mesh(mesh.devices.reshape(N_Y, N_X, N_CORE, N_REP), RED + ("rep",))
    placed = (P(RED, "rep"), P(RED + ("rep",), None), P("rep", None), P(), P(), P(), P(), P())
    return jax.shard_map(
        body, mesh=grid, in_specs=placed, out_specs=P(RED, "rep"), check_vma=False
    )
```

```python
import functools

import jax
import jax.numpy as jnp
from jax import lax
from jax.experimental import pallas as pl
from jax.experimental.pallas import tpu as pltpu
from jax.sharding import Mesh, PartitionSpec as P

SUB = 64
N_Y, N_X, N_CORE, N_REP = 4, 4, 2, 8
N_RED = N_Y * N_X * N_CORE
RED = ("y", "x", "core")
STRIDE = {"x": N_CORE, "y": N_CORE * N_X}
ORDER = (("x", "y"), ("y", "x"))
MASKS = ((1, 3), (3, 1))
MIB = 1024 * 1024


def pairs(turn, mask):
    return [(i, i ^ (mask * STRIDE[ORDER[i % 2][turn]])) for i in range(N_RED)]


def where_am_i():
    return (lax.axis_index("y") * N_X + lax.axis_index("x")) * N_CORE + lax.axis_index("core")


def pack_kernel(first_ref, amp_ref, *out_refs):
    part, tile = out_refs[0].shape[1:]
    for stream in range(2):
        core = lax.axis_index("core") ^ stream
        home = where_am_i() ^ stream
        for far in range(2):
            for sub in range(2):
                if stream:
                    out_ref = out_refs[4 + far].at[pl.ds(8 * sub, 8)]
                else:
                    out_ref = out_refs[2 * far + sub]
                for i in range(8):
                    bits = (far, i >> 2, (i >> 1) & 1, i & 1)
                    one = bits[0] * MASKS[sub][0] ^ bits[1] * MASKS[sub][1]
                    two = bits[2] * MASKS[sub][0] ^ bits[3] * MASKS[sub][1]
                    offs = [
                        one * STRIDE[axes[0]] ^ two * STRIDE[axes[1]] for axes in ORDER
                    ]
                    target = home ^ jnp.where(core == 0, offs[0], offs[1])
                    cols = pl.ds(pl.multiple_of(first_ref[0, target], tile), tile)
                    out_ref[i] = amp_ref[part * sub : part * (sub + 1), cols]


def pack(amplitudes, tile_perm, tile):
    rows = amplitudes.shape[0]
    vmem = pl.BlockSpec(memory_space=pltpu.VMEM)
    shape = jax.ShapeDtypeStruct((8, rows // 2, tile), amplitudes.dtype)
    both = jax.ShapeDtypeStruct((16, rows // 2, tile), amplitudes.dtype)
    return pl.pallas_call(
        pack_kernel,
        out_shape=[shape] * 4 + [both] * 2,
        in_specs=[pl.BlockSpec(memory_space=pltpu.SMEM), vmem],
        out_specs=[vmem] * 6,
        compiler_params=pltpu.CompilerParams(vmem_limit_bytes=24 * MIB),
        cost_estimate=pl.CostEstimate(
            flops=0, bytes_accessed=4 * amplitudes.size, transcendentals=0
        ),
    )(tile_perm * tile, amplitudes)


FORWARD = (
    ((0, 4, 8), (1, 4, 8)),
    ((0, 2, 4), (1, 2, 4), (2, 2, 4), (2, 6, 8)),
    ((0, 1, 2), (1, 1, 2), (2, 1, 2), (2, 5, 6), (3, 1, 2), (3, 3, 4), (3, 5, 6), (3, 7, 8)),
)
FINAL = (
    ((0, 0), (1, 0), (2, 0), (2, 4))
    + tuple((3, 2 * i) for i in range(4))
    + tuple((4, i) for i in range(8))
)


def of_sub(ref, sub):
    return ref.at[pl.ds(8 * sub, 8)] if ref.shape[0] == 16 else ref


def forward_kernel(plan, sub, *refs):
    *held, out_ref = refs
    at = 0
    for array, first, last in plan:
        out_ref[at : at + last - first] = of_sub(held[array], sub)[first:last]
        at += last - first


def block_at(stream, half, sub, pos):
    one = (pos >> 3) * MASKS[half][0] ^ ((pos >> 2) & 1) * MASKS[half][1]
    two = pos & 3
    if stream:
        one, two = two, one
    for f in range(16):
        bits = (f & 1, (f >> 1) & 1, (f >> 2) & 1, f >> 3)
        here = bits[0] * MASKS[sub][0] ^ bits[1] * MASKS[sub][1]
        there = bits[2] * MASKS[sub][0] ^ bits[3] * MASKS[sub][1]
        if (here, there) == (one, two):
            return FINAL[f]


def dot_tiles(stream, group, held, b_ref, lhs):
    part = held[0].shape[1]
    width = b_ref.shape[1] // N_REP
    rep = lax.axis_index("rep")
    for half in range(2):
        for pos in range(16):
            for sub in range(2):
                array, index = block_at(stream, half, sub, pos)
                row = (2 * pos + sub) * part
                lhs[row : row + part, :] = of_sub(held[5 * sub + array], sub)[index]
        for k in range(2):
            source = (2 * group + half + 4 * k) ^ rep
            b = b_ref[:, pl.ds(pl.multiple_of(source * width, width), width)]
            cols = slice(k * width, (k + 1) * width)
            yield half, cols, jnp.dot(lhs[...], b, preferred_element_type=jnp.float32)


def encode(x, out_ref, cols):
    n = x.shape[0]
    parts = [x[i : i + 16] for i in range(0, n, 16)]
    peak = jnp.abs(parts[0])
    for part in parts[1:]:
        peak = jnp.maximum(peak, jnp.abs(part))
    exponent = jnp.floor(jnp.log2(jnp.maximum(peak, 1e-30))) + 1.0
    scale = jnp.exp2(15.0 - exponent)
    for i, part in enumerate(parts):
        code = jnp.clip(jnp.round(part * scale), -32767.0, 32767.0)
        out_ref[16 * i : 16 * (i + 1), cols] = code.astype(jnp.int32).astype(jnp.int16)
    out_ref[n : n + 16, cols] = exponent.astype(jnp.int32).astype(jnp.int16)


def decode(ref, first, rows, cols=slice(None)):
    n = ref.shape[0] - 16
    exponent = ref[n : n + 16].astype(jnp.int32).astype(jnp.float32)
    scale = jnp.exp2(exponent - 15.0)
    parts = [
        ref[i : i + 16].astype(jnp.int32).astype(jnp.float32) * scale
        for i in range(first, first + rows, 16)
    ]
    return jnp.concatenate(parts, axis=0)


def away_kernel(group, *refs):
    *held, b_ref, out_ref, lhs = refs
    for half, cols, out in dot_tiles(1, group, held, b_ref, lhs):
        encode(out, out_ref.at[half], cols)


def home_kernel(group, *refs):
    *held, b_ref, out_ref, lhs = refs
    for half, cols, out in dot_tiles(0, group, held, b_ref, lhs):
        out_ref[half, :, cols] = out


def merge_kernel(home, arrived, far0, far1, near0, near1):
    n = near0.shape[0]
    for half, (far, near) in enumerate(((far0, near0), (far1, near1))):
        other = arrived.at[half]
        near[...] = home[half, :n] + decode(other, 0, n)
        encode(home[half, n:] + decode(other, n, n), far, slice(None))


def in_vmem(kernel, shapes, *args, scratch=(), limit=24):
    vmem = pl.BlockSpec(memory_space=pltpu.VMEM)
    return pl.pallas_call(
        kernel,
        out_shape=[jax.ShapeDtypeStruct(*shape) for shape in shapes],
        in_specs=[vmem] * len(args),
        out_specs=[vmem] * len(shapes),
        scratch_shapes=scratch,
        compiler_params=pltpu.CompilerParams(vmem_limit_bytes=limit * MIB),
        cost_estimate=pl.CostEstimate(flops=0, bytes_accessed=0, transcendentals=0),
    )(*args)


def step_kernel(keep0, keep1, got0, got1, far0, far1, near0, near1):
    n = near0.shape[0]
    for keep, got, far, near in ((keep0, got0, far0, near0), (keep1, got1, far1, near1)):
        near[...] = keep[:n] + decode(got, 0, n)
        encode(keep[n:] + decode(got, n, n), far, slice(None))


def join_kernel(keep0, keep1, got0, got1, *outs):
    rows = outs[0].shape[0]
    quarter = keep0.shape[1]
    for k, out in enumerate(outs):
        part = slice(k * rows, (k + 1) * rows)
        out[:, :quarter] = keep0[part] + decode(got0, k * rows, rows)
        out[:, quarter:] = keep1[part] + decode(got1, k * rows, rows)


def sum_kernel(a, b, c, d, left, right):
    n = left.shape[1]
    left[...] = (a[:, :n] + b[:, :n]) + (c[:, :n] + d[:, :n])
    right[...] = (a[:, n:] + b[:, n:]) + (c[:, n:] + d[:, n:])


def energy_kernel(occ_index, occ_energy, block_sizes, slab_irrep, virt_energy, out_ref):
    rows, columns = out_ref.shape
    tile = occ_index.shape[2]
    red, rep = where_am_i(), lax.axis_index("rep")
    row = lax.broadcasted_iota(jnp.int32, (rows, columns), 0)
    column = lax.broadcasted_iota(jnp.int32, (1, columns), 1)
    pair, first = red * rows // (tile * tile), red * rows % (tile * tile) // tile
    left = jnp.zeros((rows, columns), jnp.float32)
    for i in range(rows // tile):
        left = jnp.where(row // tile == i, occ_energy[occ_index[pair, 0, first + i]], left)
    right = jnp.zeros((rows, columns), jnp.float32)
    for j in range(tile):
        right = jnp.where(row % tile == j, occ_energy[occ_index[pair, 1, j]], right)
    start = 0
    for h in range(block_sizes.shape[0]):
        start += jnp.where(h < slab_irrep[0], block_sizes[h], 0)
    e_a = jnp.zeros((1, columns), jnp.float32)
    for a in range(columns // SUB):
        e_a = jnp.where(column // SUB == a, virt_energy[start + rep * (columns // SUB) + a], e_a)
    e_b = jnp.zeros((1, columns), jnp.float32)
    for b in range(SUB):
        e_b = jnp.where(column % SUB == b, virt_energy[start + b], e_b)
    out_ref[...] = (left + right) - (e_a + e_b)


def energy_gap(rows, columns, *args):
    return pl.pallas_call(
        energy_kernel,
        out_shape=jax.ShapeDtypeStruct((rows, columns), jnp.float32),
        in_specs=[pl.BlockSpec(memory_space=pltpu.SMEM)] * len(args),
        out_specs=pl.BlockSpec(memory_space=pltpu.VMEM),
        cost_estimate=pl.CostEstimate(flops=0, bytes_accessed=0, transcendentals=0),
    )(*args)


def body(
    amplitudes, integrals, tile_perm, occ_index, occ_energy, block_sizes, slab_irrep, virt_energy
):
    rows = amplitudes.shape[0]
    tile = integrals.shape[0]
    columns = integrals.shape[1] // N_REP
    m, quarter = 16 * rows, 2 * columns

    def stage(n):
        return [((n + 16, quarter), jnp.int16)] * 2 + [((n, quarter), jnp.float32)] * 2

    lhs = [pltpu.VMEM((m, tile), amplitudes.dtype)]
    block = ((8, rows // 2, tile), amplitudes.dtype)
    swap = [(0, 1), (1, 0)]
    packed = pack(amplitudes, tile_perm, tile)
    packed = list(packed[:4]) + [lax.ppermute(t, "core", swap) for t in (packed[5], packed[4])]
    held = [[[packed[0]], [packed[1]]], [[packed[5]], [packed[5]]]]
    sends = [packed[2:4], [None, None]]
    for step in range(4):
        turn = step // 2
        for stream in range(2):
            for sub in range(2):
                if step or stream:
                    plan = FORWARD[step - 1] if step else ((0, 0, 8),)
                    held_now = held[stream][sub] if step else [packed[4]]
                    (sends[stream][sub],) = in_vmem(
                        functools.partial(forward_kernel, plan, sub), [block], *held_now
                    )
                got = lax.ppermute(sends[stream][sub], RED, pairs(turn, MASKS[sub][step % 2]))
                held[stream][sub].append(got)
    home = [
        in_vmem(
            functools.partial(home_kernel, group),
            [((2, m, quarter), jnp.float32)],
            *held[0][0],
            *held[0][1],
            integrals,
            scratch=lhs,
        )[0]
        for group in range(2)
    ]
    held[1][0][4], held[1][1][4], home = lax.optimization_barrier(
        (held[1][0][4], held[1][1][4], home)
    )
    arrived = []
    for group in range(2):
        (away,) = in_vmem(
            functools.partial(away_kernel, group),
            [((2, m + 16, quarter), jnp.int16)],
            *held[1][0],
            *held[1][1],
            integrals,
            scratch=lhs,
        )
        arrived.append(lax.ppermute(away, "core", swap))
    keeps, gots = [], []
    for group in range(2):
        far0, far1, *near = in_vmem(merge_kernel, stage(m // 2), home[group], arrived[group])
        keeps.append(near)
        gots.append([lax.ppermute(far, RED, pairs(0, MASKS[h][0])) for h, far in enumerate((far0, far1))])
    keeps[1], occ_energy = lax.optimization_barrier((keeps[1], occ_energy))
    gap = energy_gap(
        rows, columns, occ_index, occ_energy, block_sizes, slab_irrep, virt_energy
    )
    gots[0], gap = lax.optimization_barrier((gots[0], gap))
    last, more = [], []
    for group in range(2):
        far0, far1, *near = in_vmem(step_kernel, stage(m // 4), *keeps[group], *gots[group])
        last.append(near)
        more.append([lax.ppermute(far, RED, pairs(0, MASKS[h][1])) for h, far in enumerate((far0, far1))])
    blocks = []
    for group in range(2):
        mine, *sends = in_vmem(join_kernel, [((rows, 2 * quarter), jnp.float32)] * 4, *last[group], *more[group])
        gots = [lax.ppermute(send, RED, pairs(1, k + 1)) for k, send in enumerate(sends)]
        blocks += in_vmem(sum_kernel, [((rows, quarter), jnp.float32)] * 2, mine, *gots)
    gots = [
        lax.ppermute(blocks[k], "rep", [(i, i ^ k) for i in range(N_REP)]) for k in range(1, 4)
    ]
    mine, send = in_vmem(sum_kernel, [((rows, columns), jnp.float32)] * 2, blocks[0], *gots)
    got = lax.ppermute(send, "rep", [(i, i ^ 4) for i in range(N_REP)])
    return (mine + got) / gap


def solution(mesh):
    grid = Mesh(mesh.devices.reshape(N_Y, N_X, N_CORE, N_REP), RED + ("rep",))
    placed = (P(RED, "rep"), P(RED + ("rep",), None), P("rep", None), P(), P(), P(), P(), P())
    return jax.shard_map(
        body, mesh=grid, in_specs=placed, out_specs=P(RED, "rep"), check_vma=False
    )
```

```python
import functools

import jax
import jax.numpy as jnp
from jax import lax
from jax.experimental import pallas as pl
from jax.experimental.pallas import tpu as pltpu
from jax.sharding import Mesh, PartitionSpec as P

SUB = 64
N_Y, N_X, N_CORE, N_REP = 4, 4, 2, 8
N_RED = N_Y * N_X * N_CORE
RED = ("y", "x", "core")
STRIDE = {"x": N_CORE, "y": N_CORE * N_X}
ORDER = (("x", "y"), ("y", "x"))
MASKS = ((1, 3), (3, 1))
MIB = 1024 * 1024


def pairs(turn, mask):
    return [(i, i ^ (mask * STRIDE[ORDER[i % 2][turn]])) for i in range(N_RED)]


def where_am_i():
    return (lax.axis_index("y") * N_X + lax.axis_index("x")) * N_CORE + lax.axis_index("core")


def pack_kernel(first_ref, amp_ref, *out_refs):
    part, tile = out_refs[0].shape[1:]
    for stream in range(2):
        core = lax.axis_index("core") ^ stream
        home = where_am_i() ^ stream
        for far in range(2):
            for sub in range(2):
                if stream:
                    out_ref = out_refs[4 + far].at[pl.ds(8 * sub, 8)]
                else:
                    out_ref = out_refs[2 * far + sub]
                for i in range(8):
                    bits = (far, i >> 2, (i >> 1) & 1, i & 1)
                    one = bits[0] * MASKS[sub][0] ^ bits[1] * MASKS[sub][1]
                    two = bits[2] * MASKS[sub][0] ^ bits[3] * MASKS[sub][1]
                    offs = [
                        one * STRIDE[axes[0]] ^ two * STRIDE[axes[1]] for axes in ORDER
                    ]
                    target = home ^ jnp.where(core == 0, offs[0], offs[1])
                    cols = pl.ds(pl.multiple_of(first_ref[0, target], tile), tile)
                    out_ref[i] = amp_ref[part * sub : part * (sub + 1), cols]


def pack(amplitudes, tile_perm, tile):
    rows = amplitudes.shape[0]
    vmem = pl.BlockSpec(memory_space=pltpu.VMEM)
    shape = jax.ShapeDtypeStruct((8, rows // 2, tile), amplitudes.dtype)
    both = jax.ShapeDtypeStruct((16, rows // 2, tile), amplitudes.dtype)
    return pl.pallas_call(
        pack_kernel,
        out_shape=[shape] * 4 + [both] * 2,
        in_specs=[pl.BlockSpec(memory_space=pltpu.SMEM), vmem],
        out_specs=[vmem] * 6,
        compiler_params=pltpu.CompilerParams(vmem_limit_bytes=24 * MIB),
        cost_estimate=pl.CostEstimate(
            flops=0, bytes_accessed=4 * amplitudes.size, transcendentals=0
        ),
    )(tile_perm * tile, amplitudes)


FORWARD = (
    ((0, 4, 8), (1, 4, 8)),
    ((0, 2, 4), (1, 2, 4), (2, 2, 4), (2, 6, 8)),
    ((0, 1, 2), (1, 1, 2), (2, 1, 2), (2, 5, 6), (3, 1, 2), (3, 3, 4), (3, 5, 6), (3, 7, 8)),
)
FINAL = (
    ((0, 0), (1, 0), (2, 0), (2, 4))
    + tuple((3, 2 * i) for i in range(4))
    + tuple((4, i) for i in range(8))
)


def of_sub(ref, sub):
    return ref.at[pl.ds(8 * sub, 8)] if ref.shape[0] == 16 else ref


def forward_kernel(plan, sub, *refs):
    *held, out_ref = refs
    at = 0
    for array, first, last in plan:
        out_ref[at : at + last - first] = of_sub(held[array], sub)[first:last]
        at += last - first


def block_at(stream, half, sub, pos):
    one = (pos >> 3) * MASKS[half][0] ^ ((pos >> 2) & 1) * MASKS[half][1]
    two = pos & 3
    if stream:
        one, two = two, one
    for f in range(16):
        bits = (f & 1, (f >> 1) & 1, (f >> 2) & 1, f >> 3)
        here = bits[0] * MASKS[sub][0] ^ bits[1] * MASKS[sub][1]
        there = bits[2] * MASKS[sub][0] ^ bits[3] * MASKS[sub][1]
        if (here, there) == (one, two):
            return FINAL[f]


def dot_tiles(stream, group, held, b_ref, lhs):
    part = held[0].shape[1]
    width = b_ref.shape[1] // N_REP
    rep = lax.axis_index("rep")
    for half in range(2):
        for pos in range(16):
            for sub in range(2):
                array, index = block_at(stream, half, sub, pos)
                row = (2 * pos + sub) * part
                lhs[row : row + part, :] = of_sub(held[5 * sub + array], sub)[index]
        for k in range(2):
            source = (2 * group + half + 4 * k) ^ rep
            b = b_ref[:, pl.ds(pl.multiple_of(source * width, width), width)]
            cols = slice(k * width, (k + 1) * width)
            yield half, cols, jnp.dot(lhs[...], b, preferred_element_type=jnp.float32)


def encode(x, out_ref, cols):
    n = x.shape[0]
    parts = [x[i : i + 16] for i in range(0, n, 16)]
    peak = jnp.abs(parts[0])
    for part in parts[1:]:
        peak = jnp.maximum(peak, jnp.abs(part))
    exponent = jnp.floor(jnp.log2(jnp.maximum(peak, 1e-30))) + 1.0
    scale = jnp.exp2(15.0 - exponent)
    for i, part in enumerate(parts):
        code = jnp.clip(jnp.round(part * scale), -32767.0, 32767.0)
        out_ref[16 * i : 16 * (i + 1), cols] = code.astype(jnp.int32).astype(jnp.int16)
    out_ref[n : n + 16, cols] = exponent.astype(jnp.int32).astype(jnp.int16)


def decode(ref, first, rows, cols=slice(None)):
    n = ref.shape[0] - 16
    exponent = ref[n : n + 16].astype(jnp.int32).astype(jnp.float32)
    scale = jnp.exp2(exponent - 15.0)
    parts = [
        ref[i : i + 16].astype(jnp.int32).astype(jnp.float32) * scale
        for i in range(first, first + rows, 16)
    ]
    return jnp.concatenate(parts, axis=0)


def away_kernel(group, *refs):
    *held, b_ref, out_ref, lhs = refs
    for half, cols, out in dot_tiles(1, group, held, b_ref, lhs):
        encode(out, out_ref.at[half], cols)


def home_kernel(group, *refs):
    *held, b_ref, out_ref, lhs = refs
    for half, cols, out in dot_tiles(0, group, held, b_ref, lhs):
        out_ref[half, :, cols] = out


def far_kernel(home, arrived, far0, far1):
    n = home.shape[1] // 2
    for half, far in enumerate((far0, far1)):
        encode(home[half, n:] + decode(arrived.at[half], n, n), far, slice(None))


def near_kernel(home, arrived, after, near0, near1):
    n = home.shape[1] // 2
    for half, near in enumerate((near0, near1)):
        near[...] = home[half, :n] + decode(arrived.at[half], 0, n)


def in_vmem(kernel, shapes, *args, scratch=(), limit=24):
    vmem = pl.BlockSpec(memory_space=pltpu.VMEM)
    return pl.pallas_call(
        kernel,
        out_shape=[jax.ShapeDtypeStruct(*shape) for shape in shapes],
        in_specs=[vmem] * len(args),
        out_specs=[vmem] * len(shapes),
        scratch_shapes=scratch,
        compiler_params=pltpu.CompilerParams(vmem_limit_bytes=limit * MIB),
        cost_estimate=pl.CostEstimate(flops=0, bytes_accessed=0, transcendentals=0),
    )(*args)


def step_kernel(keep, got, far, near):
    n = near.shape[0]
    near[...] = keep[:n] + decode(got, 0, n)
    encode(keep[n:] + decode(got, n, n), far, slice(None))


def join_kernel(keep0, keep1, got0, got1, *outs):
    rows = outs[0].shape[0]
    quarter = keep0.shape[1]
    for k, out in enumerate(outs):
        part = slice(k * rows, (k + 1) * rows)
        out[:, :quarter] = keep0[part] + decode(got0, k * rows, rows)
        out[:, quarter:] = keep1[part] + decode(got1, k * rows, rows)


def sum_kernel(a, b, c, d, left, right):
    n = left.shape[1]
    left[...] = (a[:, :n] + b[:, :n]) + (c[:, :n] + d[:, :n])
    right[...] = (a[:, n:] + b[:, n:]) + (c[:, n:] + d[:, n:])


def energy_kernel(occ_index, occ_energy, block_sizes, slab_irrep, virt_energy, out_ref):
    rows, columns = out_ref.shape
    tile = occ_index.shape[2]
    red, rep = where_am_i(), lax.axis_index("rep")
    row = lax.broadcasted_iota(jnp.int32, (rows, columns), 0)
    column = lax.broadcasted_iota(jnp.int32, (1, columns), 1)
    pair, first = red * rows // (tile * tile), red * rows % (tile * tile) // tile
    left = jnp.zeros((rows, columns), jnp.float32)
    for i in range(rows // tile):
        left = jnp.where(row // tile == i, occ_energy[occ_index[pair, 0, first + i]], left)
    right = jnp.zeros((rows, columns), jnp.float32)
    for j in range(tile):
        right = jnp.where(row % tile == j, occ_energy[occ_index[pair, 1, j]], right)
    start = 0
    for h in range(block_sizes.shape[0]):
        start += jnp.where(h < slab_irrep[0], block_sizes[h], 0)
    e_a = jnp.zeros((1, columns), jnp.float32)
    for a in range(columns // SUB):
        e_a = jnp.where(column // SUB == a, virt_energy[start + rep * (columns // SUB) + a], e_a)
    e_b = jnp.zeros((1, columns), jnp.float32)
    for b in range(SUB):
        e_b = jnp.where(column % SUB == b, virt_energy[start + b], e_b)
    out_ref[...] = (left + right) - (e_a + e_b)


def energy_gap(rows, columns, *args):
    return pl.pallas_call(
        energy_kernel,
        out_shape=jax.ShapeDtypeStruct((rows, columns), jnp.float32),
        in_specs=[pl.BlockSpec(memory_space=pltpu.SMEM)] * len(args),
        out_specs=pl.BlockSpec(memory_space=pltpu.VMEM),
        compiler_params=pltpu.CompilerParams(vmem_limit_bytes=8 * MIB),
        cost_estimate=pl.CostEstimate(flops=0, bytes_accessed=0, transcendentals=0),
    )(*args)


def body(
    amplitudes, integrals, tile_perm, occ_index, occ_energy, block_sizes, slab_irrep, virt_energy
):
    rows = amplitudes.shape[0]
    tile = integrals.shape[0]
    columns = integrals.shape[1] // N_REP
    m, quarter = 16 * rows, 2 * columns

    def stage(n):
        return [((n + 16, quarter), jnp.int16)] * 2 + [((n, quarter), jnp.float32)] * 2

    lhs = [pltpu.VMEM((m, tile), amplitudes.dtype)]
    block = ((8, rows // 2, tile), amplitudes.dtype)
    swap = [(0, 1), (1, 0)]
    packed = pack(amplitudes, tile_perm, tile)
    packed = list(packed[:4]) + [lax.ppermute(t, "core", swap) for t in (packed[5], packed[4])]
    held = [[[packed[0]], [packed[1]]], [[packed[5]], [packed[5]]]]
    sends = [packed[2:4], [None, None]]
    for step in range(4):
        turn = step // 2
        for stream in range(2):
            for sub in range(2):
                if step or stream:
                    plan = FORWARD[step - 1] if step else ((0, 0, 8),)
                    held_now = held[stream][sub] if step else [packed[4]]
                    (sends[stream][sub],) = in_vmem(
                        functools.partial(forward_kernel, plan, sub), [block], *held_now
                    )
                got = lax.ppermute(sends[stream][sub], RED, pairs(turn, MASKS[sub][step % 2]))
                held[stream][sub].append(got)
    home = [
        in_vmem(
            functools.partial(home_kernel, group),
            [((2, m, quarter), jnp.float32)],
            *held[0][0],
            *held[0][1],
            integrals,
            scratch=lhs,
        )[0]
        for group in range(2)
    ]
    held[1][0][4], held[1][1][4], home = lax.optimization_barrier(
        (held[1][0][4], held[1][1][4], home)
    )
    arrived = []
    for group in range(2):
        (away,) = in_vmem(
            functools.partial(away_kernel, group),
            [((2, m + 16, quarter), jnp.int16)],
            *held[1][0],
            *held[1][1],
            integrals,
            scratch=lhs,
        )
        arrived.append(lax.ppermute(away, "core", swap))
    keeps, gots = [], []
    for group in range(2):
        fars = in_vmem(far_kernel, stage(m // 2)[:2], home[group], arrived[group])
        gots.append([lax.ppermute(far, RED, pairs(0, MASKS[h][0])) for h, far in enumerate(fars)])
        keeps.append(in_vmem(near_kernel, stage(m // 2)[2:], home[group], arrived[group], fars[1]))
    last, more = [], []
    for group in range(2):
        last.append([])
        more.append([])
        for half in range(2):
            far, near = in_vmem(
                step_kernel, stage(m // 4)[1:3], keeps[group][half], gots[group][half]
            )
            last[group].append(near)
            more[group].append(lax.ppermute(far, RED, pairs(0, MASKS[half][1])))
    blocks = []
    for group in range(2):
        mine, *sends = in_vmem(join_kernel, [((rows, 2 * quarter), jnp.float32)] * 4, *last[group], *more[group])
        gots = [lax.ppermute(send, RED, pairs(1, k + 1)) for k, send in enumerate(sends)]
        blocks += in_vmem(sum_kernel, [((rows, quarter), jnp.float32)] * 2, mine, *gots)
    gots = [
        lax.ppermute(blocks[k], "rep", [(i, i ^ k) for i in range(N_REP)]) for k in range(1, 4)
    ]
    mine, send = in_vmem(sum_kernel, [((rows, columns), jnp.float32)] * 2, blocks[0], *gots)
    got = lax.ppermute(send, "rep", [(i, i ^ 4) for i in range(N_REP)])
    gap = energy_gap(
        rows, columns, occ_index, occ_energy, block_sizes, slab_irrep, virt_energy
    )
    return (mine + got) / gap


def solution(mesh):
    grid = Mesh(mesh.devices.reshape(N_Y, N_X, N_CORE, N_REP), RED + ("rep",))
    placed = (P(RED, "rep"), P(RED + ("rep",), None), P("rep", None), P(), P(), P(), P(), P())
    return jax.shard_map(
        body, mesh=grid, in_specs=placed, out_specs=P(RED, "rep"), check_vma=False
    )
```
